512 devices in a mesh: seq: 16 (over z_hi, y), kvh: 8 (over x, core), ans: 4 (over z_lo).
Axes of the slice: x: 4, y: 8, z: 8 (z_hi: 2, z_lo: 4; z = z_hi * 4 + z_lo), core: 2. Of those that a mesh axis runs over, the one named last changes fastest.
Arguments:
- query_pre: bfloat16 [2048, 8192], P('seq', ('kvh', 'ans')), may hold values from -128 to 128
- key_pre: bfloat16 [2048, 1024], P('seq', 'kvh'), may hold values from -128 to 128
- value_pre: bfloat16 [2048, 1024], P('seq', 'kvh'), may hold values from -6 to 6
- grad_pre: bfloat16 [2048, 8192], P('seq', ('kvh', 'ans')), may hold values from -6 to 6
- query_ans: bfloat16 [16, 512, 8192], P('seq', 'ans', 'kvh'), may hold values from -128 to 128
- key_ans: bfloat16 [16, 512, 1024], P('seq', 'ans', 'kvh'), may hold values from -6 to 6
- value_ans: bfloat16 [16, 512, 1024], P('seq', 'ans', 'kvh'), may hold values from -6 to 6
- grad_ans: bfloat16 [16, 512, 8192], P('seq', 'ans', 'kvh'), may hold values from -6 to 6
- lengths: int32 [16], replicated, may hold values from 1 to 512, 5120 in all
Outputs:
- prefix_out: bfloat16 [2048, 8192], P('seq', ('kvh', 'ans'))
- prefix_qgrad: bfloat16 [2048, 8192], P('seq', ('kvh', 'ans'))
- prefix_kgrad: bfloat16 [2048, 1024], P('seq', 'kvh')
- prefix_vgrad: bfloat16 [2048, 1024], P('seq', 'kvh')
- answer_out: bfloat16 [16, 512, 8192], P('seq', 'ans', 'kvh')
- answer_qgrad: bfloat16 [16, 512, 8192], P('seq', 'ans', 'kvh')
- answer_kgrad: bfloat16 [16, 512, 1024], P('seq', 'ans', 'kvh')
- answer_vgrad: bfloat16 [16, 512, 1024], P('seq', 'ans', 'kvh')
The draws below stay inside these ranges and needn't reach their ends.
Inputs may be any that keep to these rules, and one draw needn't show every extreme that they name: Answer a's first lengths[a] positions are real, the rest padding; in every draw some answer fills all 512 positions.
All inputs are finite; a program needn't handle non-finite values.
Results may differ from the reference program's by a relative error of at most 0.0095.
Values may be sent and summed in bfloat16 or wider, within the bound.
A program may use at most 64 MiB of HBM per device.

```python
import math
import jax
import jax.numpy as jnp
import numpy as np
from jax import lax

DH = 128
QH = 64
KVH = 8
PREFIX = 2048
ANSLEN = 512
ANSWERS = 16


def rough(key, rows, width, spread):
    key_val, key_row = jax.random.split(key)
    values = jnp.clip(jax.random.normal(key_val, (rows, width), jnp.float32), -6.0, 6.0)
    scales = jnp.exp(jax.random.uniform(key_row, (rows, 1), jnp.float32, -spread, spread))
    return values * scales


def draw_query_pre(key, part):
    key = jax.random.fold_in(key, 11)
    values = rough(key, PREFIX, QH * DH, 0.0)
    return values.astype(jnp.bfloat16)


def draw_query_ans(key, part):
    key = jax.random.fold_in(key, 17)
    values = rough(key, ANSWERS * ANSLEN, QH * DH, 0.0)
    return values.reshape(ANSWERS, ANSLEN, QH * DH).astype(jnp.bfloat16)


def draw_key_pre(key, part):
    key = jax.random.fold_in(key, 13)
    values = rough(key, PREFIX, KVH * DH, 0.0)
    return values.astype(jnp.bfloat16)


def levels(rng, shape, shards, low, high):
    level = 1.0
    for axis_at, shards_of in shards:
        steps = jax.random.uniform(jax.random.fold_in(jax.random.fold_in(rng, 6), axis_at), (shards_of,), jnp.float32, low / len(shards), high / len(shards))
        level = level * jnp.repeat(jnp.exp(steps), shape[axis_at] // shards_of).reshape((-1,) + (1,) * (len(shape) - 1 - axis_at))
    return level


def split_up(amount, total, bound, slope):
    loads = [(1 << 20) // math.isqrt(standing ** slope) + 1 for standing in range(2, amount + 1)]
    rest, given = total - bound - (amount - 1), [1] * (amount - 1)
    while rest > 0:
        candidates = [i for i in range(amount - 1) if given[i] < bound]
        pool, left = sum([loads[i] for i in candidates]), rest
        for i in candidates:
            more = min(bound - given[i], max(1, left * loads[i] // pool), rest)
            given[i] = given[i] + more
            rest = rest - more
    return np.array([bound] + given)


def ragged_sizes(stream_key, count, total, bound, skew):
    if count == 2:
        one = jax.random.randint(stream_key, (), max(1, total - bound), min(bound, total - 1) + 1)
        return jnp.stack([one, total - one])
    sizes = jnp.asarray(split_up(count, total, bound, skew), jnp.int32)
    pairs = (count - 1) // 2
    donor, receiver = sizes[1:1 + 2 * pairs:2], sizes[2:2 + 2 * pairs:2]
    room = jnp.minimum(donor - 1, bound - receiver)
    moved = jax.random.randint(jax.random.fold_in(stream_key, 1), (pairs,), 0, 1 << 20) % (room + 1)
    sizes = sizes.at[1:1 + 2 * pairs:2].set(donor - moved).at[2:2 + 2 * pairs:2].set(receiver + moved)
    return sizes[jax.random.permutation(jax.random.fold_in(stream_key, 2), count)]


def bell_draw(own_key, shape, scale, most, cuts=(), held_as=jnp.bfloat16):
    values = jax.random.normal(own_key, shape, jnp.float32) * scale
    if len(cuts) > 0:
        values = levels(own_key, shape, cuts, -0.22, 0.18) * values
    return jnp.clip(values, min=-most, max=most).astype(held_as)


def setup_inputs(seed: int = 0) -> dict:
    key_list = jax.random.split(jax.random.key(seed), 10)
    query_pre = draw_query_pre(jax.random.fold_in(key_list[9], 71), 0)
    key_pre = draw_key_pre(jax.random.fold_in(key_list[9], 71), 0)
    value_pre = bell_draw(key_list[2], (PREFIX, KVH * DH), 1.0, 6.0, ((0, 16), (1, 8)))
    grad_pre = bell_draw(key_list[3], (PREFIX, QH * DH), 1.0, 6.0, ((0, 16), (1, 32)))
    query_ans = draw_query_ans(jax.random.fold_in(key_list[9], 71), 0)
    key_ans = bell_draw(key_list[5], (ANSWERS, ANSLEN, KVH * DH), 1.0, 6.0, ((0, 16), (1, 4), (2, 8)))
    value_ans = bell_draw(key_list[6], (ANSWERS, ANSLEN, KVH * DH), 1.0, 6.0, ((0, 16), (1, 4), (2, 8)))
    grad_ans = bell_draw(key_list[7], (ANSWERS, ANSLEN, QH * DH), 1.0, 6.0, ((0, 16), (1, 4), (2, 8)))
    lengths = ragged_sizes(key_list[8], ANSWERS, ANSWERS * ANSLEN * 5 // 8, ANSLEN, 2).astype(jnp.int32)
    return dict(query_pre=query_pre, key_pre=key_pre, value_pre=value_pre, grad_pre=grad_pre, query_ans=query_ans, key_ans=key_ans, value_ans=value_ans, grad_ans=grad_ans, lengths=lengths)


def attend(queries, key_rows, value_rows, out_grads, positions, open_cols):
    total_rows, width = queries.shape
    block = math.gcd(total_rows, 512)
    count = total_rows // block
    factor = 1.0 / math.sqrt(width)
    columns = jnp.arange(key_rows.shape[0], dtype=jnp.int32)

    def block_step(totals, pieces):
        grad_keys, grad_values = totals
        q_block, g_block, pos_block = pieces
        scores = jnp.dot(q_block, key_rows.T, preferred_element_type=jnp.float32) * factor
        visible = (columns[None, :] < open_cols) | (columns[None, :] - open_cols <= pos_block[:, None])
        scores = jnp.where(visible, scores, -jnp.inf)
        weights = jax.nn.softmax(scores, axis=-1)
        weights_low = weights.astype(jnp.bfloat16)
        result = jnp.dot(weights_low, value_rows, preferred_element_type=jnp.float32)
        dweights = jnp.dot(g_block, value_rows.T, preferred_element_type=jnp.float32)
        row_dot = lax.optimization_barrier(jnp.sum(g_block.astype(jnp.float32) * result, axis=-1, keepdims=True))
        dscores = (weights * (dweights - row_dot)).astype(jnp.bfloat16)
        qgrad = jnp.dot(dscores, key_rows, preferred_element_type=jnp.float32) * factor
        grad_keys = grad_keys + jnp.dot(dscores.T, q_block, preferred_element_type=jnp.float32) * factor
        grad_values = grad_values + jnp.dot(weights_low.T, g_block, preferred_element_type=jnp.float32)
        return ((grad_keys, grad_values), (result, qgrad))
    zeros = jnp.zeros(key_rows.shape, jnp.float32)
    sliced = (queries.reshape(count, block, width), out_grads.reshape(count, block, width), positions.reshape(count, block))
    (grad_keys, grad_values), (results, qgrads) = lax.scan(block_step, (zeros, zeros), sliced)
    return (results.reshape(total_rows, width), qgrads.reshape(total_rows, width), grad_keys, grad_values)

def reference(query_pre, key_pre, value_pre, grad_pre, query_ans, key_ans, value_ans, grad_ans, lengths):
    group = QH // KVH
    prefix_queries = query_pre.reshape(PREFIX, KVH, group * DH).transpose(1, 0, 2).reshape(KVH, PREFIX * group, DH)
    prefix_grads = grad_pre.reshape(PREFIX, KVH, group * DH).transpose(1, 0, 2).reshape(KVH, PREFIX * group, DH)
    prefix_keys = key_pre.reshape(PREFIX, KVH, DH).transpose(1, 0, 2)
    prefix_values = value_pre.reshape(PREFIX, KVH, DH).transpose(1, 0, 2)
    prefix_positions = jnp.arange(PREFIX * group, dtype=jnp.int32) // group

    def prefix_head(pieces):
        queries, key_rows, value_rows, grads = pieces
        return attend(queries, key_rows, value_rows, grads, prefix_positions, 0)
    pre_result, pre_qgrad, pre_kgrad, pre_vgrad = lax.map(prefix_head, (prefix_queries, prefix_keys, prefix_values, prefix_grads))
    answer_queries = query_ans.reshape(ANSWERS, ANSLEN, KVH, group * DH).transpose(0, 2, 1, 3).reshape(ANSWERS * KVH, ANSLEN * group, DH)
    answer_grads = grad_ans.reshape(ANSWERS, ANSLEN, KVH, group * DH).transpose(0, 2, 1, 3).reshape(ANSWERS * KVH, ANSLEN * group, DH)
    answer_keys = key_ans.reshape(ANSWERS, ANSLEN, KVH, DH).transpose(0, 2, 1, 3).reshape(ANSWERS * KVH, ANSLEN, DH)
    answer_values = value_ans.reshape(ANSWERS, ANSLEN, KVH, DH).transpose(0, 2, 1, 3).reshape(ANSWERS * KVH, ANSLEN, DH)
    positions = jnp.arange(ANSLEN * group, dtype=jnp.int32) // group

    def answer_head(pieces):
        queries, grads, own_keys, own_values, which = pieces
        head_slot = which % KVH
        answer_slot = which // KVH
        live_rows = (positions < lengths[answer_slot]).astype(jnp.float32)
        key_rows = jnp.concatenate([prefix_keys[head_slot], own_keys], 0)
        value_rows = jnp.concatenate([prefix_values[head_slot], own_values], 0)
        masked = (grads * live_rows[:, None]).astype(jnp.bfloat16)
        result, qgrad, kgrad, vgrad = attend(queries, key_rows, value_rows, masked, positions, PREFIX)
        return (result * live_rows[:, None], qgrad, kgrad, vgrad)
    indices = jnp.arange(ANSWERS * KVH, dtype=jnp.int32)
    ans_result, ans_qgrad, ans_kgrad, ans_vgrad = lax.map(answer_head, (answer_queries, answer_grads, answer_keys, answer_values, indices))
    kgrad_total = pre_kgrad + ans_kgrad[:, :PREFIX].reshape(ANSWERS, KVH, PREFIX, DH).sum(0)
    vgrad_total = pre_vgrad + ans_vgrad[:, :PREFIX].reshape(ANSWERS, KVH, PREFIX, DH).sum(0)
    prefix_out = pre_result.reshape(KVH, PREFIX, group * DH).transpose(1, 0, 2).reshape(PREFIX, QH * DH).astype(jnp.bfloat16)
    prefix_qgrad = pre_qgrad.reshape(KVH, PREFIX, group * DH).transpose(1, 0, 2).reshape(PREFIX, QH * DH).astype(jnp.bfloat16)
    prefix_kgrad = kgrad_total.transpose(1, 0, 2).reshape(PREFIX, KVH * DH).astype(jnp.bfloat16)
    prefix_vgrad = vgrad_total.transpose(1, 0, 2).reshape(PREFIX, KVH * DH).astype(jnp.bfloat16)
    answer_out = ans_result.reshape(ANSWERS, KVH, ANSLEN, group * DH).transpose(0, 2, 1, 3).reshape(ANSWERS, ANSLEN, QH * DH).astype(jnp.bfloat16)
    answer_qgrad = ans_qgrad.reshape(ANSWERS, KVH, ANSLEN, group * DH).transpose(0, 2, 1, 3).reshape(ANSWERS, ANSLEN, QH * DH).astype(jnp.bfloat16)
    answer_kgrad = ans_kgrad[:, PREFIX:].reshape(ANSWERS, KVH, ANSLEN, DH).transpose(0, 2, 1, 3).reshape(ANSWERS, ANSLEN, KVH * DH).astype(jnp.bfloat16)
    answer_vgrad = ans_vgrad[:, PREFIX:].reshape(ANSWERS, KVH, ANSLEN, DH).transpose(0, 2, 1, 3).reshape(ANSWERS, ANSLEN, KVH * DH).astype(jnp.bfloat16)
    return (prefix_out, prefix_qgrad, prefix_kgrad, prefix_vgrad, answer_out, answer_qgrad, answer_kgrad, answer_vgrad)
```

```python
import functools
import math

import jax
import jax.numpy as jnp
from jax import lax
from jax.experimental import pallas as pl
from jax.experimental.pallas import tpu as pltpu
from jax.sharding import PartitionSpec as P

MESH = pl.DeviceIdType.MESH
F32, BF16 = jnp.float32, jnp.bfloat16
DH = 128
FACTOR = 1.0 / math.sqrt(DH)
SCALE = FACTOR * math.log2(math.e)
HIDDEN = -1e30
RA, RP = 1024, 256
R = RA + RP


def nn(a, b):
    return lax.dot_general(a, b, (((1,), (0,)), ((), ())), preferred_element_type=F32)


def tn(a, b):
    return lax.dot_general(a, b, (((0,), (0,)), ((), ())), preferred_element_type=F32)


def turn(x):
    return x.astype(F32).T


def kernel(
    qp, kp, vp, gp, qa, ka, va, ga, lengths,
    po, pq, pk, pv, ao, aq, ak, av,
    qin, gin, q_t, q_r, g_t, gs_t, gs_r, k_all, v_all, own, s_all, s_own, top, total, e_all, e_own, ds_all, ds_own,
    o_t, rowdot, gk_s, gk_r, gv_s, gv_r, acc_k, acc_v, part_k, part_v, got_k, got_v, fin, ga_own, ga_s,
    ga_r,
    in_sem, kz_ss, kz_rs, k_ss, k_rs, va_ss, va_rs, v_ss, v_rs, own_ss, own_rs, gk_ss, gk_rs, gv_ss, gv_rs,
    two_ss, two_rs, fin_ss, fin_rs, ga_ss, ga_rs,
):
    seq, q = lax.axis_index("seq"), lax.axis_index("ans")
    zh, y = lax.div(seq, 8), lax.rem(seq, 8)
    z = zh * 4 + q
    wrap = lambda i: lax.rem(i + 8, 8)
    at_y = lambda i: {"seq": zh * 8 + i, "ans": q}
    at_z = lambda i: {"seq": lax.div(i, 4) * 8 + y, "ans": lax.rem(i, 4)}
    peers = (lambda i: at_y(wrap(y + i)), lambda i: at_z(wrap(z + i)))

    def remote(src, dst, send, recv, dev):
        return pltpu.make_async_remote_copy(
            src_ref=src, dst_ref=dst, send_sem=send, recv_sem=recv, device_id=dev, device_id_type=MESH
        )

    loads = [
        pltpu.make_async_copy(qa.at[0], qin.at[:, pl.ds(0, RA)], in_sem.at[0]),
        pltpu.make_async_copy(qp, qin.at[:, pl.ds(RA, RP)], in_sem.at[1]),
        pltpu.make_async_copy(ga.at[0], gin.at[:, pl.ds(0, RA)], in_sem.at[2]),
        pltpu.make_async_copy(gp, gin.at[:, pl.ds(RA, RP)], in_sem.at[3]),
        pltpu.make_async_copy(kp, k_all.at[zh, y], in_sem.at[4]),
        pltpu.make_async_copy(vp.at[pl.ds(q * 32, 32)], v_all.at[zh, y, q], in_sem.at[5]),
        pltpu.make_async_copy(ka.at[0], own.at[q, 0], in_sem.at[6]),
        pltpu.make_async_copy(va.at[0], own.at[q, 1], in_sem.at[7]),
    ]
    for copy in loads:
        copy.start()

    barrier = pltpu.get_barrier_semaphore()
    for i in range(1, 8):
        for peer in peers:
            pl.semaphore_signal(barrier, inc=1, device_id=peer(i), device_id_type=MESH)
    pl.semaphore_wait(barrier, 14)

    half = (zh, 1 - zh)
    far = lax.rem(seq + 8, 16)
    steps = (1, -1, 2, -2)

    def key_copy(h, stage, n, came=False):
        sign, hop = (1 - 2 * (n % 2)), steps[n]
        back = (0 if stage == 1 else 2 * sign) + (hop if came else 0)
        at = k_all.at[half[h], wrap(y - back)]
        if stage == 2 and n >= 2:
            at = k_all.at[half[h], wrap(y - back), pl.ds(64 * (n % 2), 64)]
        src = kp if (stage == 1 and h == 0 and not came) else at
        return remote(src, at, k_ss.at[h, stage - 1, n], k_rs.at[h, stage - 1, n], peers[0](hop))

    def cross(i, to):
        return remote(kp, k_all.at[zh, y], kz_ss.at[i], kz_rs.at[0], {"seq": far, "ans": to})

    crossing = [(0, (3, 2)), (3, (0, 1))]
    for who, targets in crossing:
        @pl.when(q == who)
        def _():
            for i, to in enumerate(targets):
                cross(i, to).start()

    def quarter(i):
        return remote(
            vp.at[pl.ds(q * 32, 32)], v_all.at[zh, y, q], va_ss.at[i], va_rs.at[i], peers[0](i)
        )

    for i in (4, 3, -3, 2, -2, 1, -1):
        quarter(i % 8).start()
    for n in (2, 3, 0, 1):
        key_copy(0, 1, n).start()

    def value_copy(stage, n, came=False):
        sign, hop = (1 - 2 * (n % 2)), steps[n]
        at = wrap(z - ((0 if stage == 1 else 2 * sign) + (hop if came else 0)))
        block = v_all.at[lax.div(at, 4), :, lax.rem(at, 4)]
        if stage == 2 and n >= 2:
            block = v_all.at[lax.div(at, 4), pl.ds(4 * (n % 2), 4), lax.rem(at, 4)]
        return remote(block, block, v_ss.at[stage - 1, n], v_rs.at[stage - 1, n], peers[1](hop))

    def own_copy(j, side, to):
        return remote(
            (ka, va)[side].at[0], own.at[j, side], own_ss.at[to, side], own_rs.at[j, side], {"seq": seq, "ans": to}
        )

    for to in range(1, 4):
        @pl.when(q < to)
        def _():
            for side in range(2):
                own_copy(q, side, to).start()

    def drain_gather():
        for stage in range(1, 3):
            for n in range(4):
                for h in range(2):
                    key_copy(h, stage, n).wait_send()
                value_copy(stage, n).wait_send()
        for who, targets in crossing:
            @pl.when(q == who)
            def _():
                for i, to in enumerate(targets):
                    cross(i, to).wait_send()
        for i in range(1, 8):
            quarter(i).wait_send()
        for to in range(1, 4):
            @pl.when(q < to)
            def _():
                for side in range(2):
                    own_copy(q, side, to).wait_send()

    for copy in loads:
        copy.wait()
    lane = lax.rem(lax.broadcasted_iota(jnp.int32, (1, R), 1), 128)
    live = ((q * 128 + lane) < lengths[seq]) | (lax.broadcasted_iota(jnp.int32, (1, R), 1) >= RA)
    live = jnp.where(live, 1.0, 0.0)
    for h in range(R // 128):
        cols = slice(h * 128, h * 128 + 128)
        q_r[cols, :] = qin[:, cols]
        q_t[:, cols] = turn(qin[:, cols]).astype(BF16)
        g_t[:, cols] = (turn(gin[:, cols]) * live[:, cols]).astype(BF16)
    top[...] = jnp.full(top.shape, HIDDEN, F32)

    remote(kp, k_all.at[half[1], y], kz_ss.at[0], kz_rs.at[0], {"seq": far, "ans": q}).wait_recv()
    for n in (2, 3, 0, 1):
        key_copy(1, 1, n).start()

    def scores(j):
        keys = k_all[:, j].reshape(256, DH)
        s = nn(keys, q_t[:, :RA])
        s_all[:, j, :, :RA] = s.reshape(2, 128, RA)
        top[:, :RA] = jnp.maximum(top[:, :RA], s.reshape(32, 8, RA).max(0))
        s = nn(keys, q_t[:, RA:]).reshape(2, 128, RP)
        at_key = (
            lax.broadcasted_iota(jnp.int32, (2, 128, RP), 0) * 1024
            + j * 128
            + lax.broadcasted_iota(jnp.int32, (2, 128, RP), 1)
        )
        at_row = seq * 128 + lax.rem(lax.broadcasted_iota(jnp.int32, (2, 128, RP), 2), 128)
        s = jnp.where(at_key <= at_row, s, HIDDEN)
        s_all[:, j, :, RA:] = s
        top[:, RA:] = jnp.maximum(top[:, RA:], s.reshape(32, 8, RP).max(0))

    def hand_on(h):
        for n in (2, 3):
            key_copy(h, 1, n, came=True).wait_recv()
            key_copy(h, 2, n - 2).start()
            key_copy(h, 2, n).start()

    hand_on(0)
    for i in range(1, 8):
        src = wrap(y - i)
        remote(
            v_all.at[zh, src, q], v_all.at[zh, src, q], va_ss.at[i], va_rs.at[i], peers[0](i)
        ).wait_recv()
    for n in (2, 3, 0, 1):
        value_copy(1, n).start()
    scores(y)
    hand_on(1)
    for n in range(2):
        for h in range(2):
            key_copy(h, 1, n, came=True).wait_recv()
    for n in range(4):
        scores(wrap(y - steps[n]))
    for n in (2, 3):
        value_copy(1, n, came=True).wait_recv()
        value_copy(2, n - 2).start()
        value_copy(2, n).start()
    for n in range(4):
        for h in range(2):
            key_copy(h, 2, n, came=True).wait_recv()
    for n in (3, -3, 4):
        scores(wrap(y + n))

    def own_scores(j, _):
        s = nn(own[j, 0], q_t[:, :RA])
        key = lax.broadcasted_iota(jnp.int32, (128, RA), 0) + j * 128
        row = lax.rem(lax.broadcasted_iota(jnp.int32, (128, RA), 1), 128) + q * 128
        s = jnp.where(key <= row, s, HIDDEN)
        s_own[j] = s
        top[:, :RA] = jnp.maximum(top[:, :RA], s.reshape(16, 8, RA).max(0))
        return 0

    for j in range(3):
        @pl.when(q > j)
        def _():
            for side in range(2):
                own_copy(j, side, q).wait_recv()
    lax.fori_loop(0, q + 1, own_scores, 0)

    best = top[...].max(0, keepdims=True)
    top[0:1, :] = best
    total[...] = jnp.zeros_like(total)
    o_t[...] = jnp.zeros_like(o_t)

    def own_exp(j, _):
        e = jnp.exp2((s_own[j] - top[0:1, :RA]) * SCALE)
        total[:, :RA] += e.reshape(16, 8, RA).sum(0)
        e = e.astype(BF16)
        e_own[j] = e
        o_t[:, :RA] += tn(own[j, 1], e)
        return 0

    lax.fori_loop(0, q + 1, own_exp, 0)

    def exps(j, _):
        e = jnp.exp2((s_all[:, j].reshape(256, R) - top[0:1, :]) * SCALE)
        total[...] += e.reshape(32, 8, R).sum(0)
        e_all[:, j] = e.astype(BF16).reshape(2, 4, 32, R)
        return 0

    lax.fori_loop(0, 8, exps, 0)
    inverse = 1.0 / total[...].sum(0, keepdims=True)
    for h in range(R // 128):
        cols = slice(h * 128, h * 128 + 128)
        g = (g_t[:, cols].astype(F32) * inverse[:, cols]).astype(BF16)
        gs_t[:, cols] = g
        gs_r[cols, :] = turn(g).astype(BF16)

    def value_pair(j):
        return nn(e_all[:, j].reshape(256, R), gs_r[...]).reshape(2, 128, DH)

    def key_part(at):
        hi, lo = lax.div(at, 4), lax.rem(at, 4)
        dp = nn(v_all[hi, :, lo].reshape(256, DH), gs_t[...])
        e = e_all[hi, :, lo].reshape(256, R).astype(F32)
        ds = (e * (dp - rowdot[...])).astype(BF16)
        ds_all[hi, :, lo] = ds.reshape(8, 32, R)
        return nn(ds, q_r[...]).reshape(2, 128, DH)

    values = (0, y, value_pair, gv_s, gv_r, gv_ss, gv_rs, 1, z, acc_v, part_v, got_v, 1)
    keys = (1, z, key_part, gk_s, gk_r, gk_ss, gk_rs, 0, y, acc_k, part_k, got_k, 0)

    hops = {4: 2, 3: 1, 2: 2, 1: 1}

    def grad_copy(ring, d, k):
        axis, _, _, out, came, ss, rs = ring[:7]
        src, dst = out.at[d, k - 1], came.at[d, k - 1]
        if k == 4:
            src, dst = src.at[d], dst.at[d]
        return remote(src, dst, ss.at[d, k - 1], rs.at[d, k - 1], peers[axis]((1 - 2 * d) * hops[k]))

    def send_first(ring):
        axis, me, part, out = ring[:4]
        piece = part(wrap(me + 4)).astype(BF16)
        for d in range(2):
            out[d, 3, d] = piece[d]
            grad_copy(ring, d, 4).start()
        send_plain(ring, 3)

    def send_plain(ring, k):
        axis, me, part, out = ring[:4]
        for d in range(2):
            out[d, k - 1] = part(wrap(me + (1 - 2 * d) * k)).astype(BF16)
            grad_copy(ring, d, k).start()

    def send_second(ring):
        axis, me, part, out, came = ring[:5]
        pieces = [part(wrap(me + (1 - 2 * d) * 2)) for d in range(2)]
        for d in range(2):
            grad_copy(ring, d, 3).wait_recv()
            grad_copy(ring, d, 4).wait_recv()
            piece = pieces[d] + came[d, 2].astype(F32)
            out[d, 1, d] = (piece[d] + came[d, 3, d].astype(F32)).astype(BF16)
            out[d, 1, 1 - d] = piece[1 - d].astype(BF16)
            grad_copy(ring, d, 2).start()

    def add_own(ring):
        acc = ring[9]
        acc[...] = ring[2](ring[1]).reshape(acc.shape)

    def two_copy(ring, i):
        axis, me, _, sent, got, n = ring[7:]
        return remote(sent.at[wrap(me + i)], got.at[me], two_ss.at[n, i], two_rs.at[n, i], peers[axis](i))

    def exchange(ring):
        came, acc, sent = ring[4], ring[9], ring[10]
        whole = acc[...]
        for d in range(2):
            for k in range(2):
                grad_copy(ring, d, k + 1).wait_recv()
                whole = whole + came[d, k].astype(F32).reshape(acc.shape)
        acc[...] = whole
        sent[...] = whole.astype(BF16)
        for i in (4, 3, -3, 2, -2, 1, -1):
            two_copy(ring, i % 8).start()

    def fin_copy(n, i):
        other = lax.rem(q + i, 4)
        return remote(fin.at[n, q], fin.at[n, q], fin_ss.at[n, i], fin_rs.at[n, i], {"seq": seq, "ans": other})

    def finish(ring):
        axis, me, acc, sent, got, n = ring[7:]
        piece = acc[me]
        for i in range(1, 8):
            src = wrap(me - i)
            remote(
                sent.at[src], got.at[src], two_ss.at[n, i], two_rs.at[n, i], peers[axis](i)
            ).wait_recv()
            piece = piece + got[src].astype(F32)
        fin[n, q] = (piece * (FACTOR if n == 0 else 1.0)).astype(BF16)
        for i in range(1, 4):
            fin_copy(n, i).start()

    send_first(values)

    for n in range(2):
        value_copy(1, n, came=True).wait_recv()
    for n in range(4):
        value_copy(2, n, came=True).wait_recv()

    for c in range(R // 256):
        cols = slice(c * 256, c * 256 + 256)
        o = o_t[:, cols] + tn(v_all[...].reshape(2048, DH), e_all[:, :, :, :, cols].reshape(2048, 256))
        o = o * inverse[:, cols]
        rowdot[:, cols] = (gs_t[:, cols].astype(F32) * o).sum(0, keepdims=True)
        o_t[:, cols] = o * live[:, cols]

    send_first(keys)
    send_plain(values, 1)
    send_plain(keys, 1)
    send_second(values)
    add_own(values)
    add_own(keys)
    send_second(keys)

    def ans_copy(j, src):
        return remote(
            ga_s.at[j], ga_r.at[src], ga_ss.at[j], ga_rs.at[src], {"seq": seq, "ans": j}
        )

    def own_grads(j):
        e = e_own[j]
        dv = nn(e, gs_r[:RA, :])
        dp = nn(own[j, 1], gs_t[:, :RA])
        ds = (e.astype(F32) * (dp - rowdot[:, :RA])).astype(BF16)
        ds_own[j] = ds
        return nn(ds, q_r[:RA, :]), dv

    def send_own(j, _):
        dk, dv = own_grads(j)
        ga_s[j, 0] = dk.astype(BF16)
        ga_s[j, 1] = dv.astype(BF16)
        ans_copy(j, q).start()
        return 0

    lax.fori_loop(0, q, send_own, 0)
    exchange(values)
    dk, dv = own_grads(q)
    ga_own[0], ga_own[1] = dk, dv

    def rows_out(of_answers, of_prompt):
        for h in range(R // 128):
            tile = o_t[:, h * 128 : h * 128 + 128].T.astype(BF16)
            if h < RA // 128:
                of_answers[0, :, h * 128 : h * 128 + 128] = tile
            else:
                of_prompt[:, h * 128 - RA : h * 128 - RA + 128] = tile

    rows_out(ao, po)
    exchange(keys)
    finish(values)

    o_t[...] = tn(k_all[...].reshape(2048, DH), ds_all[...].reshape(2048, R))

    def own_query(j, _):
        o_t[:, :RA] += tn(own[j, 0], ds_own[j])
        return 0

    lax.fori_loop(0, q + 1, own_query, 0)
    o_t[...] = o_t[...] * FACTOR
    finish(keys)
    rows_out(aq, pq)

    for src in range(1, 4):
        @pl.when(q < src)
        def _():
            remote(
                ga_s.at[0], ga_r.at[src], ga_ss.at[0], ga_rs.at[src], {"seq": seq, "ans": q}
            ).wait_recv()
            ga_own[...] += ga_r[src].astype(F32)

    ak[0] = (ga_own[0] * FACTOR).astype(BF16)
    av[0] = ga_own[1].astype(BF16)

    drain_gather()
    for ring in (values, keys):
        for d in range(2):
            for k in range(1, 5):
                grad_copy(ring, d, k).wait_send()
        for i in range(1, 8):
            two_copy(ring, i).wait_send()
    for j in range(3):
        @pl.when(j < q)
        def _():
            ans_copy(j, q).wait_send()
    for n, out in ((1, pv), (0, pk)):
        for i in range(1, 4):
            src = lax.rem(q - i + 4, 4)
            remote(
                fin.at[n, src], fin.at[n, src], fin_ss.at[n, i], fin_rs.at[n, i], {"seq": seq, "ans": src}
            ).wait_recv()
        out[...] = fin[n].reshape(128, DH)
        for i in range(1, 4):
            fin_copy(n, i).wait_send()


def hand_out(*refs):
    sem = refs[16]
    copies = [pltpu.make_async_copy(refs[i], refs[8 + i], sem.at[i]) for i in range(8)]
    for copy in copies:
        copy.start()
    for copy in copies:
        copy.wait()


def body(query_pre, key_pre, value_pre, grad_pre, query_ans, key_ans, value_ans, grad_ans, lengths):
    shapes = [query_pre, query_pre, key_pre, value_pre, query_ans, query_ans, key_ans, value_ans]
    any_spec = pl.BlockSpec(memory_space=pl.ANY)
    vm = pltpu.VMEM
    dma = pltpu.SemaphoreType.DMA
    outs = pl.pallas_call(
        kernel,
        out_shape=[vm(x.shape, BF16) for x in shapes],
        in_specs=[any_spec] * 8 + [pl.BlockSpec(memory_space=pltpu.SMEM)],
        out_specs=[pl.BlockSpec(memory_space=vm)] * 8,
        scratch_shapes=[
            vm((128, R), BF16), vm((128, R), BF16),
            vm((DH, R), BF16), vm((R, DH), BF16),
            vm((DH, R), BF16), vm((DH, R), BF16), vm((R, DH), BF16),
            vm((2, 8, 128, DH), BF16), vm((2, 8, 4, 32, DH), BF16), vm((4, 2, 128, DH), BF16),
            vm((2, 8, 128, R), F32), vm((4, 128, RA), F32), vm((8, R), F32), vm((8, R), F32),
            vm((2, 8, 4, 32, R), BF16), vm((4, 128, RA), BF16),
            vm((2, 8, 4, 32, R), BF16), vm((4, 128, RA), BF16),
            vm((DH, R), F32), vm((1, R), F32),
            vm((2, 4, 2, 128, DH), BF16), vm((2, 4, 2, 128, DH), BF16),
            vm((2, 4, 2, 128, DH), BF16), vm((2, 4, 2, 128, DH), BF16),
            vm((8, 32, DH), F32), vm((8, 32, DH), F32),
            vm((8, 32, DH), BF16), vm((8, 32, DH), BF16), vm((8, 32, DH), BF16), vm((8, 32, DH), BF16),
            vm((2, 4, 32, DH), BF16), vm((2, 128, DH), F32),
            vm((4, 2, 128, DH), BF16), vm((4, 2, 128, DH), BF16),
            dma((8,)), dma((2,)), dma((1,)), dma((2, 2, 4)), dma((2, 2, 4)), dma((8,)), dma((8,)),
            dma((2, 4)), dma((2, 4)), dma((4, 2)), dma((4, 2)), dma((2, 4)), dma((2, 4)), dma((2, 4)), dma((2, 4)),
            dma((2, 8)), dma((2, 8)), dma((2, 4)), dma((2, 4)), dma((4,)), dma((4,)),
        ],
        compiler_params=pltpu.CompilerParams(
            collective_id=0, has_side_effects=True, vmem_limit_bytes=56 * 1024 * 1024
        ),
        cost_estimate=pl.CostEstimate(flops=5_000_000_000, bytes_accessed=3_000_000, transcendentals=3_200_000),
        name="attention",
    )(query_pre, key_pre, value_pre, grad_pre, query_ans, key_ans, value_ans, grad_ans, lengths)
    return pl.pallas_call(
        hand_out,
        out_shape=[jax.ShapeDtypeStruct(x.shape, BF16) for x in shapes],
        in_specs=[any_spec] * 8,
        out_specs=[any_spec] * 8,
        scratch_shapes=[dma((8,))],
        cost_estimate=pl.CostEstimate(flops=0, bytes_accessed=1_700_000, transcendentals=0),
        name="hand_out",
    )(*[pltpu.with_memory_space_constraint(x, vm) for x in outs])


def solution(mesh):
    rows, keys = P("seq", ("kvh", "ans")), P("seq", "kvh")
    answers = P("seq", "ans", "kvh")
    return jax.shard_map(
        body,
        mesh=mesh,
        in_specs=(rows, keys, keys, rows, answers, answers, answers, answers, P()),
        out_specs=(rows, rows, keys, keys, answers, answers, answers, answers),
        check_vma=False,
    )
```
